32 devices in a mesh: parts: 2 (over x), row: 16 (over z, y, core).
Axes of the slice: x: 2, y: 2, z: 4, core: 2. Of those that a mesh axis runs over, the one named last changes fastest.
Arguments:
- audio: bfloat16 [8388608], P(('parts', 'row')), parts along dimension 0, may hold values from -8 to 8
- templates: bfloat16 [8192, 512], P(('parts', 'row')), parts along dimension 0, may hold values from 0.025 to 4, as said below
- activations: bfloat16 [4096, 512], P(('parts', 'row')), parts along dimension 0, may hold values from 0.025 to 4, as said below
Outputs:
- h_new: bfloat16 [4096, 512], P(('parts', 'row')), parts along dimension 0
- w_new: bfloat16 [8192, 512], P(('parts', 'row')), parts along dimension 0
The draws below stay inside these ranges and needn't reach their ends.
There are 2 independent parts, one for each index of `parts`. The reference program is written for one: setup_inputs(seed, part) draws one part's arguments, and reference() takes and returns one part's arrays. A program takes and returns all parts, laid end to end along the dimension named above; each array names one. Nothing has to cross between parts.
Inputs may be any that keep to these rules, and one draw needn't show every extreme that they name: `templates`: positive entries. `activations`: positive entries.
All inputs are finite; a program needn't handle non-finite values.
Results may differ from the reference program's by a relative error of at most 0.0034.
Values may be sent and summed in bfloat16 or wider, within the bound.
A program may use at most 64 MiB of HBM per device.

```python
import math
import jax
import jax.numpy as jnp
from jax import lax

NFFT = 8192
RANK = 512
FR_DEV = 128
BINS = 4096
HOP = 2048
FRAMES = 2048
SAMPLES = 4194304
BIN_DEV = 256


def localized(key, total_rows, block_rows):
    centre_key, value_key = jax.random.split(key)
    centres = jax.random.randint(centre_key, (RANK,), 0, total_rows // block_rows)
    owner_block = (jnp.arange(total_rows, dtype=jnp.int32) // block_rows)[:, None]
    near_scale = jnp.where(owner_block == centres[None, :], 1.0, 0.05)
    base_vals = jnp.exp(jax.random.uniform(value_key, (total_rows, RANK), jnp.float32, math.log(0.5), math.log(4.0)))
    return base_vals * near_scale


def draw_audio(key, part):
    noise_key, gain_key = jax.random.split(key)
    noise_vals = jnp.clip(jax.random.normal(noise_key, (SAMPLES,), jnp.float32), -4.0, 4.0)
    seg_gain = jnp.exp(jax.random.uniform(gain_key, (SAMPLES // HOP, 1), jnp.float32, math.log(0.2), math.log(2.0)))
    return (noise_vals.reshape(SAMPLES // HOP, HOP) * seg_gain).reshape(SAMPLES).astype(jnp.bfloat16)


def draw_templates(key, part):
    values_out = localized(jax.random.fold_in(key, 11), BINS, BIN_DEV)
    return values_out.astype(jnp.bfloat16)


def draw_activations(key, part):
    values_out = localized(jax.random.fold_in(key, 23), FRAMES, FR_DEV)
    return values_out.astype(jnp.bfloat16)


def setup_inputs(seed: int = 0, part: int = 0) -> dict:
    keys = jax.random.split(jax.random.key(seed), 4)
    part_keys = jax.random.split(jax.random.fold_in(keys[3], part), 4)
    return {
        "audio": draw_audio(jax.random.fold_in(jax.random.fold_in(keys[3], part), 71), part),
        "templates": draw_templates(jax.random.fold_in(jax.random.fold_in(keys[3], part), 71), part),
        "activations": draw_activations(jax.random.fold_in(jax.random.fold_in(keys[3], part), 71), part),
    }


radix = 128

def dft_tables(length):
    inner_len = length // radix
    half_len = inner_len // 2
    outer_idx = jnp.arange(radix, dtype=jnp.int32)
    inner_idx = jnp.arange(inner_len, dtype=jnp.int32)
    upper_idx = jnp.arange(half_len, dtype=jnp.int32)
    angle_one = (outer_idx[:, None] * outer_idx[None, :] % radix).astype(jnp.float32) * (2.0 * math.pi / radix)
    section_one = jnp.concatenate([jnp.cos(angle_one), -jnp.sin(angle_one)], axis=1).astype(jnp.bfloat16)
    angle_twid = (inner_idx[:, None] * outer_idx[None, :] % length).astype(jnp.float32) * (2.0 * math.pi / length)
    angle_two = (inner_idx[:, None] * upper_idx[None, :] % inner_len).astype(jnp.float32) * (2.0 * math.pi / inner_len)
    cos_two = jnp.cos(angle_two)
    sin_two = jnp.sin(angle_two)
    upper_half = jnp.concatenate([cos_two, -sin_two], axis=1)
    lower_half = jnp.concatenate([sin_two, cos_two], axis=1)
    section_two = jnp.concatenate([upper_half, lower_half], axis=0).astype(jnp.bfloat16)
    sample_idx = jnp.arange(length, dtype=jnp.int32).astype(jnp.float32)
    hann_window = 0.5 - 0.5 * jnp.cos(sample_idx * (2.0 * math.pi / length))
    return (hann_window, section_one, jnp.cos(angle_twid), jnp.sin(angle_twid), section_two)

def magnitudes(windowed, tables_all):
    hann_window, section_one, twid_cos, twid_sin, section_two = tables_all
    frame_count = windowed.shape[0]
    length = windowed.shape[1]
    inner_len = section_two.shape[0] // 2
    half_len = inner_len // 2
    shaped = windowed.reshape(frame_count, radix, inner_len).astype(jnp.float32)
    section_out = jnp.einsum('nab,ac->nbc', shaped, section_one.astype(jnp.float32), precision=lax.Precision.HIGHEST)
    real_y = section_out[:, :, :radix]
    imag_y = section_out[:, :, radix:]
    real_z = (real_y * twid_cos + imag_y * twid_sin).astype(jnp.bfloat16)
    imag_z = (imag_y * twid_cos - real_y * twid_sin).astype(jnp.bfloat16)
    stacked = jnp.concatenate([real_z, imag_z], axis=1).astype(jnp.float32)
    second = jnp.einsum('nbk,bm->nmk', stacked, section_two.astype(jnp.float32), precision=lax.Precision.HIGHEST)
    real_x = second[:, :half_len, :]
    imag_x = second[:, half_len:, :]
    level = jnp.sqrt(real_x * real_x + imag_x * imag_x) * (16.0 / math.sqrt(length))
    return level.reshape(frame_count, half_len * radix).astype(jnp.bfloat16)

def reference(audio, templates, activations):
    tables_all = dft_tables(NFFT)
    padded = jnp.concatenate([audio, jnp.zeros((3 * HOP,), audio.dtype)])
    frame_rows = padded.reshape(FRAMES + 3, HOP)
    block_len = math.gcd(FRAMES, 512)

    def one_block(block_index):
        first_row = (block_index * block_len).astype(jnp.int32)
        window_rows = lax.dynamic_slice_in_dim(frame_rows, first_row, block_len + 3, 0)
        frames = jnp.concatenate([window_rows[offset:offset + block_len] for offset in range(4)], axis=1)
        windowed = (frames.astype(jnp.float32) * tables_all[0]).astype(jnp.bfloat16)
        return magnitudes(windowed, tables_all)
    blocks_out = lax.map(one_block, jnp.arange(FRAMES // block_len, dtype=jnp.int32))
    spectrogram = blocks_out.reshape(FRAMES, BINS)
    gram_w = jnp.dot(templates.T, templates, preferred_element_type=jnp.float32).astype(jnp.bfloat16)
    num_h = jnp.dot(spectrogram, templates, preferred_element_type=jnp.float32)
    den_h = jnp.dot(activations, gram_w, preferred_element_type=jnp.float32)
    h_new = (activations.astype(jnp.float32) * num_h / den_h).astype(jnp.bfloat16)
    gram_h = jnp.dot(h_new.T, h_new, preferred_element_type=jnp.float32).astype(jnp.bfloat16)
    num_w = jnp.dot(spectrogram.T, h_new, preferred_element_type=jnp.float32)
    den_w = jnp.dot(templates, gram_h, preferred_element_type=jnp.float32)
    w_new = (templates.astype(jnp.float32) * num_w / den_w).astype(jnp.bfloat16)
    return (h_new, w_new)
```

```python
import functools
import math

import jax
import jax.numpy as jnp
import numpy as np
from jax import lax
from jax.experimental import pallas as pl
from jax.experimental.pallas import tpu as pltpu
from jax.sharding import PartitionSpec as P

NFFT = 8192
BINS = 4096
HOP = 2048


radix = 128


def shifted(value, axis, by):
    length = lax.axis_size(axis)
    pairs = [(i, i + by) for i in range(length) if 0 <= i + by < length]
    return lax.ppermute(value, axis, pairs)


def dft_tables(length):
    inner_len = length // radix
    half_len = inner_len // 2
    outer_idx = jnp.arange(radix, dtype=jnp.int32)
    inner_idx = jnp.arange(inner_len, dtype=jnp.int32)
    upper_idx = jnp.arange(half_len, dtype=jnp.int32)
    angle_one = (outer_idx[:, None] * outer_idx[None, :] % radix).astype(jnp.float32) * (
        2.0 * math.pi / radix
    )
    section_one = jnp.concatenate([jnp.cos(angle_one), -jnp.sin(angle_one)], axis=1).astype(
        jnp.bfloat16
    )
    angle_twid = (inner_idx[:, None] * outer_idx[None, :] % length).astype(jnp.float32) * (
        2.0 * math.pi / length
    )
    angle_two = (inner_idx[:, None] * upper_idx[None, :] % inner_len).astype(jnp.float32) * (
        2.0 * math.pi / inner_len
    )
    cos_two = jnp.cos(angle_two)
    sin_two = jnp.sin(angle_two)
    upper_half = jnp.concatenate([cos_two, -sin_two], axis=1)
    lower_half = jnp.concatenate([sin_two, cos_two], axis=1)
    section_two = jnp.concatenate([upper_half, lower_half], axis=0).astype(jnp.bfloat16)
    sample_idx = jnp.arange(length, dtype=jnp.int32).astype(jnp.float32)
    hann_window = 0.5 - 0.5 * jnp.cos(sample_idx * (2.0 * math.pi / length))
    return (hann_window, section_one, jnp.cos(angle_twid), jnp.sin(angle_twid), section_two)


def magnitudes(windowed, tables_all):
    hann_window, section_one, twid_cos, twid_sin, section_two = tables_all
    frame_count = windowed.shape[0]
    length = windowed.shape[1]
    inner_len = section_two.shape[0] // 2
    half_len = inner_len // 2
    shaped = windowed.reshape(frame_count, radix, inner_len)
    section_out = jnp.einsum("nab,ac->nbc", shaped, section_one, preferred_element_type=jnp.float32)
    real_y = section_out[:, :, :radix]
    imag_y = section_out[:, :, radix:]
    real_z = (real_y * twid_cos + imag_y * twid_sin).astype(jnp.bfloat16)
    imag_z = (imag_y * twid_cos - real_y * twid_sin).astype(jnp.bfloat16)
    stacked = jnp.concatenate([real_z, imag_z], axis=1)
    second = jnp.einsum("nbk,bm->nmk", stacked, section_two, preferred_element_type=jnp.float32)
    real_x = second[:, :half_len, :]
    imag_x = second[:, half_len:, :]
    level = jnp.sqrt(real_x * real_x + imag_x * imag_x) * (16.0 / math.sqrt(length))
    return level.reshape(frame_count, half_len * radix).astype(jnp.bfloat16)


def inner_rows(left, right):
    return lax.dot_general(
        left, right, (((0,), (0,)), ((), ())), preferred_element_type=jnp.float32
    )


def refine(factor, numer, gram_low):
    denom = jnp.dot(factor, gram_low, preferred_element_type=jnp.float32)
    return (factor.astype(jnp.float32) * numer / denom).astype(jnp.bfloat16)


def own_gram(factor):
    return lax.psum(inner_rows(factor, factor), "row")


def shards(audio, templates, activations):
    frame_count = activations.shape[0]
    tables_all = dft_tables(NFFT)
    tail_audio = shifted(audio[: 3 * HOP], "row", -1)
    frame_rows = jnp.concatenate([audio, tail_audio]).reshape(frame_count + 3, HOP)
    block_len = math.gcd(frame_count, 16)

    def one_block(block_index):
        window_rows = lax.dynamic_slice_in_dim(
            frame_rows, block_index * block_len, block_len + 3, 0
        )
        frames = jnp.concatenate(
            [window_rows[offset : offset + block_len] for offset in range(4)], axis=1
        )
        windowed = (frames.astype(jnp.float32) * tables_all[0]).astype(jnp.bfloat16)
        return magnitudes(windowed, tables_all)

    blocks_out = lax.map(one_block, jnp.arange(frame_count // block_len, dtype=jnp.int32))
    spectrogram = blocks_out.reshape(frame_count, BINS)
    gram_w = lax.psum(inner_rows(templates, templates), "row").astype(jnp.bfloat16)
    columns = lax.all_to_all(spectrogram, "row", split_axis=1, concat_axis=0, tiled=True)
    num_h = lax.psum_scatter(
        jnp.dot(columns, templates, preferred_element_type=jnp.float32),
        "row",
        scatter_dimension=0,
        tiled=True,
    )
    h_new = refine(activations, num_h, gram_w)
    num_acc = inner_rows(columns, lax.all_gather(h_new, "row", axis=0, tiled=True))
    gram_h = own_gram(h_new)
    w_new = refine(templates, num_acc, gram_h.astype(jnp.bfloat16))
    return (h_new, w_new)


LINE = 4
STEP_FRAMES = 8


def host_tables():
    inner_len = NFFT // radix
    half_len = inner_len // 2
    two_pi = np.float32(2.0 * math.pi)
    outer = np.arange(radix)
    inner = np.arange(inner_len)
    upper = np.arange(half_len)
    one = (outer[:, None] * outer[None, :] % radix).astype(np.float32) * (two_pi / np.float32(radix))
    table = np.concatenate([np.cos(one), -np.sin(one)], axis=1)
    first = np.zeros((2, 2, inner_len, 2, 2 * radix), np.float32)
    for parity in range(2):
        for which in range(2):
            first[parity, which, :, which, :] = table[parity::2]
    first = first.reshape(4 * inner_len, 4 * radix)
    twid = (inner[:, None] * outer[None, :] % NFFT).astype(np.float32) * (two_pi / np.float32(NFFT))
    two = (inner[:, None] * upper[None, :] % inner_len).astype(np.float32) * (
        two_pi / np.float32(inner_len)
    )
    cos_two, sin_two = np.cos(two), np.sin(two)
    second = np.concatenate(
        [
            np.concatenate([cos_two, -sin_two], axis=1),
            np.concatenate([sin_two, cos_two], axis=1),
        ],
        axis=0,
    ).T
    samples = np.arange(NFFT).astype(np.float32)
    hann = np.float32(0.5) - np.float32(0.5) * np.cos(samples * (two_pi / np.float32(NFFT)))
    hann = hann.reshape(NFFT // radix, radix)
    return (
        jnp.asarray(np.concatenate([hann, hann], axis=0), jnp.float32),
        jnp.asarray(first).astype(jnp.bfloat16),
        jnp.asarray(np.cos(twid), jnp.float32),
        jnp.asarray(np.sin(twid), jnp.float32),
        jnp.asarray(second).astype(jnp.bfloat16),
    )


def dot(left, right, left_dim=1, right_dim=0):
    return lax.dot_general(
        left, right, (((left_dim,), (right_dim,)), ((), ())), preferred_element_type=jnp.float32
    )


def fused(
    aud, tmpl, act, hann, first, tcos, tsin, second, h_out, w_out,
    ext, halo, mag, spec, cols, wall, hall, num_h, den_h, num_w, den_w,
    halo_sems, w_send, w_recv, h_send, h_recv, x_send, x_recv,
):
    count = lax.axis_size("row")
    me = lax.axis_index("row")
    z, y, c = me // 4, (me // 2) % 2, me % 2
    frames = act.shape[0]
    bins = tmpl.shape[0]
    planes = bins // radix
    half = NFFT // radix // 2
    samples = aud.shape[0]

    def place(zz, yy, cc):
        return (zz * 2 + yy) * 2 + cc

    core_peer = place(z, y, 1 - c)
    y_peer = place(z, 1 - y, c)

    def send(src, dst, send_sem, recv_sem, device):
        return pltpu.make_async_remote_copy(
            src_ref=src,
            dst_ref=dst,
            send_sem=send_sem,
            recv_sem=recv_sem,
            device_id={"row": device},
            device_id_type=pl.DeviceIdType.MESH,
        )

    barrier = pltpu.get_barrier_semaphore()
    for d in range(1, count):
        pl.semaphore_signal(
            barrier,
            inc=1,
            device_id={"row": lax.rem(me + d, count)},
            device_id_type=pl.DeviceIdType.MESH,
        )
    pl.semaphore_wait(barrier, count - 1)

    halo_copy = send(
        aud.at[pl.ds(0, halo.shape[0])], halo, halo_sems.at[0], halo_sems.at[1],
        lax.rem(me + count - 1, count),
    )
    halo_copy.start()

    def gather(buf, rows, send_sems, recv_sems):
        def view(slot):
            return buf.at[pl.ds(pl.multiple_of(slot * rows, rows), rows)]

        def make(slot, way, device):
            return send(
                view(slot), view(slot), send_sems.at[way, slot], recv_sems.at[slot], device
            )

        def arrived(slot):
            make(slot, 0, core_peer).wait_recv()

        def each_send(slot_z, sign, act_on):
            slot = place(slot_z, y, c)
            for way, step in ((2, 1), (3, -1)):
                if sign in (0, step):

                    @pl.when((z + step >= 0) & (z + step < LINE))
                    def _():
                        act_on(make(slot, way, place(z + step, y, c)))

            act_on(make(slot, 1, y_peer))
            act_on(make(slot, 0, core_peer))

        def over_line(d, body):
            for sign in (1, -1):
                from_z = z - sign * d

                @pl.when((from_z >= 0) & (from_z < LINE))
                def _():
                    body(from_z, sign)

        def start_own():
            each_send(z, 0, lambda cp: cp.start())

        def relay_line(d):
            def body(from_z, sign):
                arrived(place(from_z, y, c))
                each_send(from_z, sign, lambda cp: cp.start())

            over_line(d, body)

        def relay_side(d):
            def body(from_z, sign):
                slot = place(from_z, 1 - y, c)
                arrived(slot)
                make(slot, 0, core_peer).start()

            if d == 0:
                body(z, 0)
            else:
                over_line(d, body)

        def finish():
            for zz in range(LINE):
                for yy in range(2):
                    arrived(place(zz, yy, 1 - c))

        def drain():
            each_send(z, 0, lambda cp: cp.wait_send())
            make(place(z, 1 - y, c), 0, core_peer).wait_send()
            for d in range(1, LINE):

                def body(from_z, sign):
                    each_send(from_z, sign, lambda cp: cp.wait_send())
                    make(place(from_z, 1 - y, c), 0, core_peer).wait_send()

                over_line(d, body)

        return start_own, relay_line, relay_side, finish, drain

    w_start, w_line, w_side, w_finish, w_drain = gather(wall, bins, w_send, w_recv)
    h_start, h_line, h_side, h_finish, h_drain = gather(hall, frames, h_send, h_recv)

    wall[pl.ds(pl.multiple_of(me * bins, bins), bins)] = tmpl[...]
    w_start()
    ext[pl.ds(0, samples)] = aud[...]

    per_frame = HOP // radix
    pairs = STEP_FRAMES // 2

    def transform(i, carry):
        base = pl.multiple_of(i * STEP_FRAMES * per_frame, STEP_FRAMES * per_frame)
        lefts = []
        for f in range(pairs):
            block = ext[pl.ds(base + per_frame * f, radix)].astype(jnp.float32) * hann[...]
            turned = block.astype(jnp.bfloat16).T
            lefts.append(jnp.concatenate([turned[: radix // 2], turned[radix // 2 :]], axis=1))
        out_one = dot(jnp.concatenate(lefts, axis=0), first[...])
        rights = []
        for f in range(pairs):
            for g in range(2):
                piece = out_one[64 * f : 64 * f + 64, 256 * g : 256 * g + 256]
                real_y = piece[:, :radix]
                imag_y = piece[:, radix:]
                real_z = (real_y * tcos[...] + imag_y * tsin[...]).astype(jnp.bfloat16)
                imag_z = (imag_y * tcos[...] - real_y * tsin[...]).astype(jnp.bfloat16)
                rights.append(jnp.concatenate([real_z, imag_z], axis=0))
        out_two = dot(second[...], jnp.concatenate(rights, axis=1))
        real_x = out_two[:half]
        imag_x = out_two[half:]
        level = jnp.sqrt(real_x * real_x + imag_x * imag_x) * (16.0 / math.sqrt(NFFT))
        for f in range(pairs):
            for g in range(2):
                j = 2 * f + g
                frame = i * STEP_FRAMES + f + pairs * g
                mag[pl.ds(pl.multiple_of(frame * half, half), half)] = level[
                    :, radix * j : radix * j + radix
                ]
        return carry

    steps = frames // STEP_FRAMES
    cut_one, cut_two = steps // 2, steps - 1
    lax.fori_loop(0, cut_one, transform, 0)
    w_line(1)
    lax.fori_loop(cut_one, cut_two, transform, 0)
    halo_copy.wait()
    tail = halo[...]
    ext[pl.ds(samples, halo.shape[0])] = jnp.where(me == count - 1, jnp.zeros_like(tail), tail)
    lax.fori_loop(cut_two, steps, transform, 0)
    w_side(0)
    w_line(2)

    def regroup(m, carry):
        spec[m] = mag[pl.ds(m, frames, stride=half), :].astype(jnp.bfloat16)
        return carry

    lax.fori_loop(0, half, regroup, 0)

    def exchange(dz, dy, dc):
        target = place(lax.rem(z + dz, LINE), lax.rem(y + dy, 2), lax.rem(c + dc, 2))
        order = (dz * 2 + dy) * 2 + dc
        return send(
            spec.at[pl.ds(target * planes, planes)],
            cols.at[:, pl.ds(pl.multiple_of(me * frames, frames), frames)],
            x_send.at[order],
            x_recv.at[me],
            target,
        )

    def each_exchange(act_on):
        for dz in (2, 1, 3, 0):
            for dy in (1, 0):
                for dc in (0, 1):
                    if dz or dy or dc:
                        act_on(exchange(dz, dy, dc))

    each_exchange(lambda cp: cp.start())
    cols[:, pl.ds(pl.multiple_of(me * frames, frames), frames)] = spec[
        pl.ds(me * planes, planes)
    ]
    w_side(1)
    w_line(3)
    w_side(2)
    w_side(3)
    w_finish()

    num_h[...] = jnp.zeros_like(num_h)
    den_h[...] = jnp.zeros_like(den_h)

    def bins_step(s, carry):
        block = wall[pl.ds(pl.multiple_of(s * bins, bins), bins)]
        left = jnp.concatenate([spec[s * planes + p] for p in range(planes)], axis=1)
        num_h[...] += dot(left, block)
        mid = dot(act[...], block, 1, 1).astype(jnp.bfloat16)
        den_h[...] += dot(mid, block)
        return carry

    lax.fori_loop(0, count, bins_step, 0)
    h_new = (act[...].astype(jnp.float32) * num_h[...] / den_h[...]).astype(jnp.bfloat16)
    h_out[...] = h_new
    hall[pl.ds(pl.multiple_of(me * frames, frames), frames)] = h_new
    h_start()
    h_line(1)
    h_side(0)
    h_line(2)
    h_side(1)
    h_line(3)
    h_side(2)
    h_side(3)
    h_finish()

    def exchanged(src):
        send(
            spec.at[pl.ds(0, planes)],
            cols.at[:, pl.ds(pl.multiple_of(src * frames, frames), frames)],
            x_send.at[0],
            x_recv.at[src],
            core_peer,
        ).wait_recv()

    for d in range(1, count):
        exchanged(lax.rem(me + d, count))

    num_w[...] = jnp.zeros_like(num_w)
    den_w[...] = jnp.zeros_like(den_w)
    chunk = 2 * frames

    def frames_step(s, carry):
        rows = pl.ds(pl.multiple_of(s * chunk, chunk), chunk)
        block = hall[rows]
        mid = dot(tmpl[...], block, 1, 1).astype(jnp.bfloat16)
        den_w[...] += dot(mid, block)
        for p in range(planes):
            num_w[pl.ds(p * radix, radix)] += dot(cols[p, rows], block, 0, 0)
        return carry

    lax.fori_loop(0, count * frames // chunk, frames_step, 0)
    w_out[...] = (tmpl[...].astype(jnp.float32) * num_w[...] / den_w[...]).astype(jnp.bfloat16)
    w_drain()
    h_drain()
    each_exchange(lambda cp: cp.wait_send())


def fused_shards(audio, templates, activations):
    count = lax.axis_size("row")
    frames, rank = activations.shape
    bins = templates.shape[0]
    tables = host_tables()
    aud = audio.reshape(audio.shape[0] // radix, radix)
    halo_rows = 3 * HOP // radix
    low, wide = jnp.bfloat16, jnp.float32
    vmem = pl.BlockSpec(memory_space=pltpu.VMEM)
    dma = pltpu.SemaphoreType.DMA
    return pl.pallas_call(
        fused,
        out_shape=(
            jax.ShapeDtypeStruct(activations.shape, low),
            jax.ShapeDtypeStruct(templates.shape, low),
        ),
        in_specs=[vmem] * 8,
        out_specs=(vmem, vmem),
        scratch_shapes=[
            pltpu.VMEM((aud.shape[0] + halo_rows, radix), low),
            pltpu.VMEM((halo_rows, radix), low),
            pltpu.VMEM((frames * BINS // radix, radix), wide),
            pltpu.VMEM((BINS // radix, frames, radix), low),
            pltpu.VMEM((bins // radix, count * frames, radix), low),
            pltpu.VMEM((count * bins, rank), low),
            pltpu.VMEM((count * frames, rank), low),
            pltpu.VMEM((frames, rank), wide),
            pltpu.VMEM((frames, rank), wide),
            pltpu.VMEM((bins, rank), wide),
            pltpu.VMEM((bins, rank), wide),
            dma((2,)),
            dma((4, count)),
            dma((count,)),
            dma((4, count)),
            dma((count,)),
            dma((count,)),
            dma((count,)),
        ],
        compiler_params=pltpu.CompilerParams(
            collective_id=0, has_side_effects=True, vmem_limit_bytes=48 * 1024 * 1024
        ),
        cost_estimate=pl.CostEstimate(
            flops=4_000_000_000, bytes_accessed=8_000_000, transcendentals=0
        ),
        name="spectral_nmf",
    )(aud, templates, activations, *tables)


def solution(mesh):
    in_specs = (P(("parts", "row")), P(("parts", "row"), None), P(("parts", "row"), None))
    out_specs = (P(("parts", "row"), None), P(("parts", "row"), None))
    body = fused_shards if mesh.shape["row"] == LINE * 4 else shards
    return jax.shard_map(body, mesh=mesh, in_specs=in_specs, out_specs=out_specs, check_vma=False)
```

```python
import functools
import math

import jax
import jax.numpy as jnp
import numpy as np
from jax import lax
from jax.experimental import pallas as pl
from jax.experimental.pallas import tpu as pltpu
from jax.sharding import PartitionSpec as P

NFFT = 8192
BINS = 4096
HOP = 2048


radix = 128


def shifted(value, axis, by):
    length = lax.axis_size(axis)
    pairs = [(i, i + by) for i in range(length) if 0 <= i + by < length]
    return lax.ppermute(value, axis, pairs)


def dft_tables(length):
    inner_len = length // radix
    half_len = inner_len // 2
    outer_idx = jnp.arange(radix, dtype=jnp.int32)
    inner_idx = jnp.arange(inner_len, dtype=jnp.int32)
    upper_idx = jnp.arange(half_len, dtype=jnp.int32)
    angle_one = (outer_idx[:, None] * outer_idx[None, :] % radix).astype(jnp.float32) * (
        2.0 * math.pi / radix
    )
    section_one = jnp.concatenate([jnp.cos(angle_one), -jnp.sin(angle_one)], axis=1).astype(
        jnp.bfloat16
    )
    angle_twid = (inner_idx[:, None] * outer_idx[None, :] % length).astype(jnp.float32) * (
        2.0 * math.pi / length
    )
    angle_two = (inner_idx[:, None] * upper_idx[None, :] % inner_len).astype(jnp.float32) * (
        2.0 * math.pi / inner_len
    )
    cos_two = jnp.cos(angle_two)
    sin_two = jnp.sin(angle_two)
    upper_half = jnp.concatenate([cos_two, -sin_two], axis=1)
    lower_half = jnp.concatenate([sin_two, cos_two], axis=1)
    section_two = jnp.concatenate([upper_half, lower_half], axis=0).astype(jnp.bfloat16)
    sample_idx = jnp.arange(length, dtype=jnp.int32).astype(jnp.float32)
    hann_window = 0.5 - 0.5 * jnp.cos(sample_idx * (2.0 * math.pi / length))
    return (hann_window, section_one, jnp.cos(angle_twid), jnp.sin(angle_twid), section_two)


def magnitudes(windowed, tables_all):
    hann_window, section_one, twid_cos, twid_sin, section_two = tables_all
    frame_count = windowed.shape[0]
    length = windowed.shape[1]
    inner_len = section_two.shape[0] // 2
    half_len = inner_len // 2
    shaped = windowed.reshape(frame_count, radix, inner_len)
    section_out = jnp.einsum("nab,ac->nbc", shaped, section_one, preferred_element_type=jnp.float32)
    real_y = section_out[:, :, :radix]
    imag_y = section_out[:, :, radix:]
    real_z = (real_y * twid_cos + imag_y * twid_sin).astype(jnp.bfloat16)
    imag_z = (imag_y * twid_cos - real_y * twid_sin).astype(jnp.bfloat16)
    stacked = jnp.concatenate([real_z, imag_z], axis=1)
    second = jnp.einsum("nbk,bm->nmk", stacked, section_two, preferred_element_type=jnp.float32)
    real_x = second[:, :half_len, :]
    imag_x = second[:, half_len:, :]
    level = jnp.sqrt(real_x * real_x + imag_x * imag_x) * (16.0 / math.sqrt(length))
    return level.reshape(frame_count, half_len * radix).astype(jnp.bfloat16)


def inner_rows(left, right):
    return lax.dot_general(
        left, right, (((0,), (0,)), ((), ())), preferred_element_type=jnp.float32
    )


def refine(factor, numer, gram_low):
    denom = jnp.dot(factor, gram_low, preferred_element_type=jnp.float32)
    return (factor.astype(jnp.float32) * numer / denom).astype(jnp.bfloat16)


def own_gram(factor):
    return lax.psum(inner_rows(factor, factor), "row")


def shards(audio, templates, activations):
    frame_count = activations.shape[0]
    tables_all = dft_tables(NFFT)
    tail_audio = shifted(audio[: 3 * HOP], "row", -1)
    frame_rows = jnp.concatenate([audio, tail_audio]).reshape(frame_count + 3, HOP)
    block_len = math.gcd(frame_count, 16)

    def one_block(block_index):
        window_rows = lax.dynamic_slice_in_dim(
            frame_rows, block_index * block_len, block_len + 3, 0
        )
        frames = jnp.concatenate(
            [window_rows[offset : offset + block_len] for offset in range(4)], axis=1
        )
        windowed = (frames.astype(jnp.float32) * tables_all[0]).astype(jnp.bfloat16)
        return magnitudes(windowed, tables_all)

    blocks_out = lax.map(one_block, jnp.arange(frame_count // block_len, dtype=jnp.int32))
    spectrogram = blocks_out.reshape(frame_count, BINS)
    gram_w = lax.psum(inner_rows(templates, templates), "row").astype(jnp.bfloat16)
    columns = lax.all_to_all(spectrogram, "row", split_axis=1, concat_axis=0, tiled=True)
    num_h = lax.psum_scatter(
        jnp.dot(columns, templates, preferred_element_type=jnp.float32),
        "row",
        scatter_dimension=0,
        tiled=True,
    )
    h_new = refine(activations, num_h, gram_w)
    num_acc = inner_rows(columns, lax.all_gather(h_new, "row", axis=0, tiled=True))
    gram_h = own_gram(h_new)
    w_new = refine(templates, num_acc, gram_h.astype(jnp.bfloat16))
    return (h_new, w_new)


LINE = 4
STEP_FRAMES = 8
W_PIECES = 2
H_PIECES = 2
EXCHANGE = ((0,), (2,), (1, 3), ())


def host_tables():
    inner_len = NFFT // radix
    half_len = inner_len // 2
    two_pi = np.float32(2.0 * math.pi)
    outer = np.arange(radix)
    inner = np.arange(inner_len)
    upper = np.arange(half_len)
    one = (outer[:, None] * outer[None, :] % radix).astype(np.float32) * (two_pi / np.float32(radix))
    table = np.concatenate([np.cos(one), -np.sin(one)], axis=1)
    first = np.zeros((2, 2, inner_len, 2, 2 * radix), np.float32)
    for parity in range(2):
        for which in range(2):
            first[parity, which, :, which, :] = table[parity::2]
    first = first.reshape(4 * inner_len, 4 * radix)
    twid = (inner[:, None] * outer[None, :] % NFFT).astype(np.float32) * (two_pi / np.float32(NFFT))
    two = (inner[:, None] * upper[None, :] % inner_len).astype(np.float32) * (
        two_pi / np.float32(inner_len)
    )
    cos_two, sin_two = np.cos(two), np.sin(two)
    second = np.concatenate(
        [
            np.concatenate([cos_two, -sin_two], axis=1),
            np.concatenate([sin_two, cos_two], axis=1),
        ],
        axis=0,
    ).T
    samples = np.arange(NFFT).astype(np.float32)
    hann = np.float32(0.5) - np.float32(0.5) * np.cos(samples * (two_pi / np.float32(NFFT)))
    hann = hann.reshape(NFFT // radix, radix)
    return (
        jnp.asarray(np.concatenate([hann, hann], axis=0), jnp.float32),
        jnp.asarray(first).astype(jnp.bfloat16),
        jnp.asarray(np.cos(twid), jnp.float32),
        jnp.asarray(np.sin(twid), jnp.float32),
        jnp.asarray(second).astype(jnp.bfloat16),
    )


def dot(left, right, left_dim=1, right_dim=0):
    return lax.dot_general(
        left, right, (((left_dim,), (right_dim,)), ((), ())), preferred_element_type=jnp.float32
    )


def fused(
    aud_in, tmpl_in, act_in, hann_in, first_in, tcos_in, tsin_in, second_in, h_out, w_out,
    act, hann, first, tcos, tsin, second,
    ext, halo, mag, spec, cols, wall, hall, num_h, den_h, num_w, den_w,
    load_sems, halo_sems, w_send, w_recv, h_send, h_recv, x_send, x_recv,
):
    count = lax.axis_size("row")
    me = lax.axis_index("row")
    z, y, c = me // 4, (me // 2) % 2, me % 2
    frames = act_in.shape[0]
    bins = tmpl_in.shape[0]
    planes = bins // radix
    half = NFFT // radix // 2
    samples = aud_in.shape[0]

    def place(zz, yy, cc):
        return (zz * 2 + yy) * 2 + cc

    core_peer = place(z, y, 1 - c)
    y_peer = place(z, 1 - y, c)

    def send(src, dst, send_sem, recv_sem, device):
        return pltpu.make_async_remote_copy(
            src_ref=src,
            dst_ref=dst,
            send_sem=send_sem,
            recv_sem=recv_sem,
            device_id={"row": device},
            device_id_type=pl.DeviceIdType.MESH,
        )

    own_bins = pl.ds(pl.multiple_of(me * bins, bins), bins)
    own_frames = pl.ds(pl.multiple_of(me * frames, frames), frames)
    loads = [
        pltpu.make_async_copy(src, dst, load_sems.at[i])
        for i, (src, dst) in enumerate(
            (
                (tmpl_in, wall.at[own_bins]),
                (aud_in, ext.at[pl.ds(0, samples)]),
                (hann_in, hann),
                (first_in, first),
                (tcos_in, tcos),
                (tsin_in, tsin),
                (second_in, second),
                (act_in, act),
            )
        )
    ]
    for load in loads:
        load.start()

    barrier = pltpu.get_barrier_semaphore()
    for d in range(1, count):
        pl.semaphore_signal(
            barrier,
            inc=1,
            device_id={"row": lax.rem(me + d, count)},
            device_id_type=pl.DeviceIdType.MESH,
        )
    pl.semaphore_wait(barrier, count - 1)

    halo_copy = send(
        aud_in.at[pl.ds(0, halo.shape[0])], halo, halo_sems.at[0], halo_sems.at[1],
        lax.rem(me + count - 1, count),
    )
    halo_copy.start()

    def gather(buf, rows, pieces, send_sems, recv_sems):
        size = rows // pieces

        def make(slot, q, way, device):
            unit = slot * pieces + q
            view = buf.at[pl.ds(pl.multiple_of(unit * size, size), size)]
            return send(view, view, send_sems.at[way, unit], recv_sems.at[unit], device)

        def arrived(slot, q):
            make(slot, q, 0, core_peer).wait_recv()

        def each_send(slot_z, q, sign, act_on):
            slot = place(slot_z, y, c)
            for way, step in ((2, 1), (3, -1)):
                if sign in (0, step):

                    @pl.when((z + step >= 0) & (z + step < LINE))
                    def _():
                        act_on(make(slot, q, way, place(z + step, y, c)))

            act_on(make(slot, q, 1, y_peer))
            act_on(make(slot, q, 0, core_peer))

        def over_line(d, body):
            if d == 0:
                body(z, 0)
                return
            for sign in (1, -1):
                from_z = z - sign * d

                @pl.when((from_z >= 0) & (from_z < LINE))
                def _():
                    body(from_z, sign)

        def start_own():
            for q in range(pieces):
                each_send(z, q, 0, lambda cp: cp.start())

        def relay_line(d):
            for q in range(pieces):

                def body(from_z, sign):
                    arrived(place(from_z, y, c), q)
                    each_send(from_z, q, sign, lambda cp: cp.start())

                over_line(d, body)

        def relay_side(d):
            for q in range(pieces):

                def body(from_z, sign):
                    slot = place(from_z, 1 - y, c)
                    arrived(slot, q)
                    make(slot, q, 0, core_peer).start()

                over_line(d, body)

        def plane(d, process):
            def body(from_z, sign):
                for q in range(pieces):
                    for yy in range(2):
                        arrived(place(from_z, yy, 1 - c), q)
                process(from_z)

            over_line(d, body)

        def drain():
            for q in range(pieces):
                for d in range(LINE):

                    def body(from_z, sign):
                        each_send(from_z, q, sign, lambda cp: cp.wait_send())
                        make(place(from_z, 1 - y, c), q, 0, core_peer).wait_send()

                    over_line(d, body)

        return start_own, relay_line, relay_side, plane, drain

    w_start, w_line, w_side, w_plane, w_drain = gather(wall, bins, W_PIECES, w_send, w_recv)
    h_start, h_line, h_side, h_plane, h_drain = gather(hall, frames, H_PIECES, h_send, h_recv)

    loads[0].wait()
    w_start()
    for load in loads[1:]:
        load.wait()

    per_frame = HOP // radix
    pairs = STEP_FRAMES // 2

    def transform(i, carry):
        base = pl.multiple_of(i * STEP_FRAMES * per_frame, STEP_FRAMES * per_frame)
        lefts = []
        for f in range(pairs):
            block = ext[pl.ds(base + per_frame * f, radix)].astype(jnp.float32) * hann[...]
            turned = block.astype(jnp.bfloat16).T
            lefts.append(jnp.concatenate([turned[: radix // 2], turned[radix // 2 :]], axis=1))
        out_one = dot(jnp.concatenate(lefts, axis=0), first[...])
        rights = []
        for f in range(pairs):
            for g in range(2):
                piece = out_one[64 * f : 64 * f + 64, 256 * g : 256 * g + 256]
                real_y = piece[:, :radix]
                imag_y = piece[:, radix:]
                real_z = (real_y * tcos[...] + imag_y * tsin[...]).astype(jnp.bfloat16)
                imag_z = (imag_y * tcos[...] - real_y * tsin[...]).astype(jnp.bfloat16)
                rights.append(jnp.concatenate([real_z, imag_z], axis=0))
        out_two = dot(second[...], jnp.concatenate(rights, axis=1))
        real_x = out_two[:half]
        imag_x = out_two[half:]
        level = jnp.sqrt(real_x * real_x + imag_x * imag_x) * (16.0 / math.sqrt(NFFT))
        for f in range(pairs):
            for g in range(2):
                j = 2 * f + g
                frame = i * STEP_FRAMES + f + pairs * g
                mag[pl.ds(pl.multiple_of(frame * half, half), half)] = level[
                    :, radix * j : radix * j + radix
                ]
        return carry

    steps = frames // STEP_FRAMES
    lax.fori_loop(0, steps - 1, transform, 0)
    halo_copy.wait()
    tail = halo[...]
    ext[pl.ds(samples, halo.shape[0])] = jnp.where(me == count - 1, jnp.zeros_like(tail), tail)
    lax.fori_loop(steps - 1, steps, transform, 0)
    w_line(1)

    def regroup(m, carry):
        spec[m] = mag[pl.ds(m, frames, stride=half), :].astype(jnp.bfloat16)
        return carry

    lax.fori_loop(0, half, regroup, 0)

    def exchange(dz, dy, dc):
        target = place(lax.rem(z + dz, LINE), lax.rem(y + dy, 2), lax.rem(c + dc, 2))
        order = (dz * 2 + dy) * 2 + dc
        return send(
            spec.at[pl.ds(target * planes, planes)],
            cols.at[:, pl.ds(pl.multiple_of(me * frames, frames), frames)],
            x_send.at[order],
            x_recv.at[me],
            target,
        )

    def each_exchange(dz, act_on):
        for dy in (1, 0):
            for dc in (0, 1):
                if dz or dy or dc:
                    act_on(exchange(dz, dy, dc))

    num_h[...] = jnp.zeros_like(num_h)
    den_h[...] = jnp.zeros_like(den_h)

    def bins_plane(zz):
        span = 4 * bins
        block = wall[pl.ds(pl.multiple_of(zz * span, span), span)]
        first_plane = zz * (4 * planes)
        left = jnp.concatenate([spec[first_plane + p] for p in range(4 * planes)], axis=1)
        mid = dot(act[...], block, 1, 1).astype(jnp.bfloat16)
        num_h[...] += dot(left, block)
        den_h[...] += dot(mid, block)

    def start_exchange(point):
        for dz in EXCHANGE[point]:
            each_exchange(dz, lambda cp: cp.start())

    start_exchange(0)
    cols[:, own_frames] = spec[pl.ds(me * planes, planes)]
    w_side(0)
    w_plane(0, bins_plane)
    w_line(2)
    start_exchange(1)
    w_side(1)
    w_plane(1, bins_plane)
    w_line(3)
    start_exchange(2)
    w_side(2)
    w_plane(2, bins_plane)
    w_side(3)
    w_plane(3, bins_plane)

    h_new = (act[...].astype(jnp.float32) * num_h[...] / den_h[...]).astype(jnp.bfloat16)
    h_out[...] = h_new
    hall[own_frames] = h_new
    h_start()
    start_exchange(3)

    def exchanged(src):
        send(
            spec.at[pl.ds(0, planes)],
            cols.at[:, pl.ds(pl.multiple_of(src * frames, frames), frames)],
            x_send.at[0],
            x_recv.at[src],
            core_peer,
        ).wait_recv()

    num_w[...] = jnp.zeros_like(num_w)
    den_w[...] = jnp.zeros_like(den_w)

    def plane_rows(zz):
        span = 4 * frames
        return pl.ds(pl.multiple_of(zz * span, span), span)

    def gram_plane(zz):
        block = hall[plane_rows(zz)]
        mid = dot(wall[own_bins], block, 1, 1).astype(jnp.bfloat16)
        den_w[...] += dot(mid, block)

    def frames_plane(zz):
        rows = plane_rows(zz)
        for p in range(planes):
            num_w[pl.ds(p * radix, radix)] += dot(cols[p, rows], hall[rows], 0, 0)

    h_line(1)
    h_side(0)
    h_line(2)
    h_plane(0, gram_plane)
    h_side(1)
    h_line(3)
    h_plane(1, gram_plane)
    h_side(2)
    h_side(3)
    for dz in (0, 1, 3, 2):
        for dy in range(2):
            for dc in range(2):
                if dz or dy or dc:
                    exchanged(place(lax.rem(z + dz, LINE), lax.rem(y + dy, 2), lax.rem(c + dc, 2)))
        if dz == 0:
            frames_plane(z)
    h_plane(2, gram_plane)
    h_plane(3, gram_plane)
    for dz in (1, 3, 2):
        frames_plane(lax.rem(z + dz, LINE))
    w_out[...] = (wall[own_bins].astype(jnp.float32) * num_w[...] / den_w[...]).astype(jnp.bfloat16)
    w_drain()
    h_drain()
    for dz in range(LINE):
        each_exchange(dz, lambda cp: cp.wait_send())


def fused_shards(audio, templates, activations):
    count = lax.axis_size("row")
    frames, rank = activations.shape
    bins = templates.shape[0]
    tables = host_tables()
    aud = audio.reshape(audio.shape[0] // radix, radix)
    halo_rows = 3 * HOP // radix
    low, wide = jnp.bfloat16, jnp.float32
    vmem = pl.BlockSpec(memory_space=pltpu.VMEM)
    dma = pltpu.SemaphoreType.DMA
    return pl.pallas_call(
        fused,
        out_shape=(
            jax.ShapeDtypeStruct(activations.shape, low),
            jax.ShapeDtypeStruct(templates.shape, low),
        ),
        in_specs=[pl.BlockSpec(memory_space=pl.ANY)] * 8,
        out_specs=(vmem, vmem),
        scratch_shapes=[
            pltpu.VMEM(activations.shape, low),
            *(pltpu.VMEM(table.shape, table.dtype) for table in tables),
            pltpu.VMEM((aud.shape[0] + halo_rows, radix), low),
            pltpu.VMEM((halo_rows, radix), low),
            pltpu.VMEM((frames * BINS // radix, radix), wide),
            pltpu.VMEM((BINS // radix, frames, radix), low),
            pltpu.VMEM((bins // radix, count * frames, radix), low),
            pltpu.VMEM((count * bins, rank), low),
            pltpu.VMEM((count * frames, rank), low),
            pltpu.VMEM((frames, rank), wide),
            pltpu.VMEM((frames, rank), wide),
            pltpu.VMEM((bins, rank), wide),
            pltpu.VMEM((bins, rank), wide),
            dma((8,)),
            dma((2,)),
            dma((4, count * W_PIECES)),
            dma((count * W_PIECES,)),
            dma((4, count * H_PIECES)),
            dma((count * H_PIECES,)),
            dma((count,)),
            dma((count,)),
        ],
        compiler_params=pltpu.CompilerParams(
            collective_id=0, has_side_effects=True, vmem_limit_bytes=60 * 1024 * 1024
        ),
        cost_estimate=pl.CostEstimate(
            flops=4_000_000_000, bytes_accessed=8_000_000, transcendentals=0
        ),
        name="spectral_nmf",
    )(aud, templates, activations, *tables)


def solution(mesh):
    in_specs = (P(("parts", "row")), P(("parts", "row"), None), P(("parts", "row"), None))
    out_specs = (P(("parts", "row"), None), P(("parts", "row"), None))
    body = fused_shards if mesh.shape["row"] == LINE * 4 else shards
    return jax.shard_map(body, mesh=mesh, in_specs=in_specs, out_specs=out_specs, check_vma=False)
```

```python
import functools
import math

import jax
import jax.numpy as jnp
import numpy as np
from jax import lax
from jax.experimental import pallas as pl
from jax.experimental.pallas import tpu as pltpu
from jax.sharding import PartitionSpec as P

NFFT = 8192
BINS = 4096
HOP = 2048


radix = 128


def shifted(value, axis, by):
    length = lax.axis_size(axis)
    pairs = [(i, i + by) for i in range(length) if 0 <= i + by < length]
    return lax.ppermute(value, axis, pairs)


def dft_tables(length):
    inner_len = length // radix
    half_len = inner_len // 2
    outer_idx = jnp.arange(radix, dtype=jnp.int32)
    inner_idx = jnp.arange(inner_len, dtype=jnp.int32)
    upper_idx = jnp.arange(half_len, dtype=jnp.int32)
    angle_one = (outer_idx[:, None] * outer_idx[None, :] % radix).astype(jnp.float32) * (
        2.0 * math.pi / radix
    )
    section_one = jnp.concatenate([jnp.cos(angle_one), -jnp.sin(angle_one)], axis=1).astype(
        jnp.bfloat16
    )
    angle_twid = (inner_idx[:, None] * outer_idx[None, :] % length).astype(jnp.float32) * (
        2.0 * math.pi / length
    )
    angle_two = (inner_idx[:, None] * upper_idx[None, :] % inner_len).astype(jnp.float32) * (
        2.0 * math.pi / inner_len
    )
    cos_two = jnp.cos(angle_two)
    sin_two = jnp.sin(angle_two)
    upper_half = jnp.concatenate([cos_two, -sin_two], axis=1)
    lower_half = jnp.concatenate([sin_two, cos_two], axis=1)
    section_two = jnp.concatenate([upper_half, lower_half], axis=0).astype(jnp.bfloat16)
    sample_idx = jnp.arange(length, dtype=jnp.int32).astype(jnp.float32)
    hann_window = 0.5 - 0.5 * jnp.cos(sample_idx * (2.0 * math.pi / length))
    return (hann_window, section_one, jnp.cos(angle_twid), jnp.sin(angle_twid), section_two)


def magnitudes(windowed, tables_all):
    hann_window, section_one, twid_cos, twid_sin, section_two = tables_all
    frame_count = windowed.shape[0]
    length = windowed.shape[1]
    inner_len = section_two.shape[0] // 2
    half_len = inner_len // 2
    shaped = windowed.reshape(frame_count, radix, inner_len)
    section_out = jnp.einsum("nab,ac->nbc", shaped, section_one, preferred_element_type=jnp.float32)
    real_y = section_out[:, :, :radix]
    imag_y = section_out[:, :, radix:]
    real_z = (real_y * twid_cos + imag_y * twid_sin).astype(jnp.bfloat16)
    imag_z = (imag_y * twid_cos - real_y * twid_sin).astype(jnp.bfloat16)
    stacked = jnp.concatenate([real_z, imag_z], axis=1)
    second = jnp.einsum("nbk,bm->nmk", stacked, section_two, preferred_element_type=jnp.float32)
    real_x = second[:, :half_len, :]
    imag_x = second[:, half_len:, :]
    level = jnp.sqrt(real_x * real_x + imag_x * imag_x) * (16.0 / math.sqrt(length))
    return level.reshape(frame_count, half_len * radix).astype(jnp.bfloat16)


def inner_rows(left, right):
    return lax.dot_general(
        left, right, (((0,), (0,)), ((), ())), preferred_element_type=jnp.float32
    )


def refine(factor, numer, gram_low):
    denom = jnp.dot(factor, gram_low, preferred_element_type=jnp.float32)
    return (factor.astype(jnp.float32) * numer / denom).astype(jnp.bfloat16)


def own_gram(factor):
    return lax.psum(inner_rows(factor, factor), "row")


def shards(audio, templates, activations):
    frame_count = activations.shape[0]
    tables_all = dft_tables(NFFT)
    tail_audio = shifted(audio[: 3 * HOP], "row", -1)
    frame_rows = jnp.concatenate([audio, tail_audio]).reshape(frame_count + 3, HOP)
    block_len = math.gcd(frame_count, 16)

    def one_block(block_index):
        window_rows = lax.dynamic_slice_in_dim(
            frame_rows, block_index * block_len, block_len + 3, 0
        )
        frames = jnp.concatenate(
            [window_rows[offset : offset + block_len] for offset in range(4)], axis=1
        )
        windowed = (frames.astype(jnp.float32) * tables_all[0]).astype(jnp.bfloat16)
        return magnitudes(windowed, tables_all)

    blocks_out = lax.map(one_block, jnp.arange(frame_count // block_len, dtype=jnp.int32))
    spectrogram = blocks_out.reshape(frame_count, BINS)
    gram_w = lax.psum(inner_rows(templates, templates), "row").astype(jnp.bfloat16)
    columns = lax.all_to_all(spectrogram, "row", split_axis=1, concat_axis=0, tiled=True)
    num_h = lax.psum_scatter(
        jnp.dot(columns, templates, preferred_element_type=jnp.float32),
        "row",
        scatter_dimension=0,
        tiled=True,
    )
    h_new = refine(activations, num_h, gram_w)
    num_acc = inner_rows(columns, lax.all_gather(h_new, "row", axis=0, tiled=True))
    gram_h = own_gram(h_new)
    w_new = refine(templates, num_acc, gram_h.astype(jnp.bfloat16))
    return (h_new, w_new)


LINE = 4
STEP_FRAMES = 8
W_PIECES = 2
H_PIECES = 2
EXCHANGE = ((), (2,), (1, 3), (0,))


def host_tables():
    inner_len = NFFT // radix
    half_len = inner_len // 2
    two_pi = np.float32(2.0 * math.pi)
    outer = np.arange(radix)
    inner = np.arange(inner_len)
    upper = np.arange(half_len)
    one = (outer[:, None] * outer[None, :] % radix).astype(np.float32) * (two_pi / np.float32(radix))
    table = np.concatenate([np.cos(one), -np.sin(one)], axis=1)
    first = np.zeros((2, 2, inner_len, 2, 2 * radix), np.float32)
    for parity in range(2):
        for which in range(2):
            first[parity, which, :, which, :] = table[parity::2]
    first = first.reshape(4 * inner_len, 4 * radix)
    twid = (inner[:, None] * outer[None, :] % NFFT).astype(np.float32) * (two_pi / np.float32(NFFT))
    two = (inner[:, None] * upper[None, :] % inner_len).astype(np.float32) * (
        two_pi / np.float32(inner_len)
    )
    cos_two, sin_two = np.cos(two), np.sin(two)
    second = np.concatenate(
        [
            np.concatenate([cos_two, -sin_two], axis=1),
            np.concatenate([sin_two, cos_two], axis=1),
        ],
        axis=0,
    ).T
    samples = np.arange(NFFT).astype(np.float32)
    hann = np.float32(0.5) - np.float32(0.5) * np.cos(samples * (two_pi / np.float32(NFFT)))
    hann = hann.reshape(NFFT // radix, radix)
    return (
        jnp.asarray(np.concatenate([hann, hann], axis=0), jnp.float32),
        jnp.asarray(first).astype(jnp.bfloat16),
        jnp.asarray(np.cos(twid), jnp.float32),
        jnp.asarray(np.sin(twid), jnp.float32),
        jnp.asarray(second).astype(jnp.bfloat16),
    )


def dot(left, right, left_dim=1, right_dim=0):
    return lax.dot_general(
        left, right, (((left_dim,), (right_dim,)), ((), ())), preferred_element_type=jnp.float32
    )


def fused(
    aud_in, tmpl_in, act_in, hann_in, first_in, tcos_in, tsin_in, second_in, h_out, w_out,
    act, hann, first, tcos, tsin, second,
    ext, halo, mag, spec, cols, wall, hall, num_h, den_h, num_w, den_w,
    load_sems, halo_sems, w_send, w_recv, h_send, h_recv, x_send, x_recv,
):
    count = lax.axis_size("row")
    me = lax.axis_index("row")
    z, y, c = me // 4, (me // 2) % 2, me % 2
    frames = act_in.shape[0]
    bins = tmpl_in.shape[0]
    planes = bins // radix
    half = NFFT // radix // 2
    samples = aud_in.shape[0]

    def place(zz, yy, cc):
        return (zz * 2 + yy) * 2 + cc

    core_peer = place(z, y, 1 - c)
    y_peer = place(z, 1 - y, c)

    def send(src, dst, send_sem, recv_sem, device):
        return pltpu.make_async_remote_copy(
            src_ref=src,
            dst_ref=dst,
            send_sem=send_sem,
            recv_sem=recv_sem,
            device_id={"row": device},
            device_id_type=pl.DeviceIdType.MESH,
        )

    own_bins = pl.ds(pl.multiple_of(me * bins, bins), bins)
    own_frames = pl.ds(pl.multiple_of(me * frames, frames), frames)
    loads = [
        pltpu.make_async_copy(src, dst, load_sems.at[i])
        for i, (src, dst) in enumerate(
            (
                (tmpl_in, wall.at[own_bins]),
                (aud_in, ext.at[pl.ds(0, samples)]),
                (hann_in, hann),
                (first_in, first),
                (tcos_in, tcos),
                (tsin_in, tsin),
                (second_in, second),
                (act_in, act),
            )
        )
    ]
    for load in loads:
        load.start()

    barrier = pltpu.get_barrier_semaphore()
    for d in range(1, count):
        pl.semaphore_signal(
            barrier,
            inc=1,
            device_id={"row": lax.rem(me + d, count)},
            device_id_type=pl.DeviceIdType.MESH,
        )
    pl.semaphore_wait(barrier, count - 1)

    halo_copy = send(
        aud_in.at[pl.ds(0, halo.shape[0])], halo, halo_sems.at[0], halo_sems.at[1],
        lax.rem(me + count - 1, count),
    )
    halo_copy.start()

    def gather(buf, rows, pieces, send_sems, recv_sems):
        size = rows // pieces

        def make(slot, q, way, device):
            unit = slot * pieces + q
            view = buf.at[pl.ds(pl.multiple_of(unit * size, size), size)]
            return send(view, view, send_sems.at[way, unit], recv_sems.at[unit], device)

        def arrived(slot, q):
            make(slot, q, 0, core_peer).wait_recv()

        def each_send(slot_z, q, sign, act_on):
            slot = place(slot_z, y, c)
            for way, step in ((2, 1), (3, -1)):
                if sign in (0, step):

                    @pl.when((z + step >= 0) & (z + step < LINE))
                    def _():
                        act_on(make(slot, q, way, place(z + step, y, c)))

            act_on(make(slot, q, 1, y_peer))
            act_on(make(slot, q, 0, core_peer))

        def over_line(d, body):
            if d == 0:
                body(z, 0)
                return
            for sign in (1, -1):
                from_z = z - sign * d

                @pl.when((from_z >= 0) & (from_z < LINE))
                def _():
                    body(from_z, sign)

        def start_own():
            for q in range(pieces):
                each_send(z, q, 0, lambda cp: cp.start())

        def relay_line(d):
            for q in range(pieces):

                def body(from_z, sign):
                    arrived(place(from_z, y, c), q)
                    each_send(from_z, q, sign, lambda cp: cp.start())

                over_line(d, body)

        def relay_side(d):
            for q in range(pieces):

                def body(from_z, sign):
                    slot = place(from_z, 1 - y, c)
                    arrived(slot, q)
                    make(slot, q, 0, core_peer).start()

                over_line(d, body)

        def plane(d, process):
            def body(from_z, sign):
                for q in range(pieces):
                    for yy in range(2):
                        arrived(place(from_z, yy, 1 - c), q)
                process(from_z)

            over_line(d, body)

        def drain():
            for q in range(pieces):
                for d in range(LINE):

                    def body(from_z, sign):
                        each_send(from_z, q, sign, lambda cp: cp.wait_send())
                        make(place(from_z, 1 - y, c), q, 0, core_peer).wait_send()

                    over_line(d, body)

        return start_own, relay_line, relay_side, plane, drain

    w_start, w_line, w_side, w_plane, w_drain = gather(wall, bins, W_PIECES, w_send, w_recv)
    h_start, h_line, h_side, h_plane, h_drain = gather(hall, frames, H_PIECES, h_send, h_recv)

    loads[0].wait()
    w_start()
    for load in loads[1:]:
        load.wait()

    per_frame = HOP // radix
    pairs = STEP_FRAMES // 2

    def transform(i, carry):
        base = pl.multiple_of(i * STEP_FRAMES * per_frame, STEP_FRAMES * per_frame)
        lefts = []
        for f in range(pairs):
            block = ext[pl.ds(base + per_frame * f, radix)].astype(jnp.float32) * hann[...]
            turned = block.astype(jnp.bfloat16).T
            lefts.append(jnp.concatenate([turned[: radix // 2], turned[radix // 2 :]], axis=1))
        out_one = dot(jnp.concatenate(lefts, axis=0), first[...])
        rights = []
        for f in range(pairs):
            for g in range(2):
                piece = out_one[64 * f : 64 * f + 64, 256 * g : 256 * g + 256]
                real_y = piece[:, :radix]
                imag_y = piece[:, radix:]
                real_z = (real_y * tcos[...] + imag_y * tsin[...]).astype(jnp.bfloat16)
                imag_z = (imag_y * tcos[...] - real_y * tsin[...]).astype(jnp.bfloat16)
                rights.append(jnp.concatenate([real_z, imag_z], axis=0))
        out_two = dot(second[...], jnp.concatenate(rights, axis=1))
        real_x = out_two[:half]
        imag_x = out_two[half:]
        level = jnp.sqrt(real_x * real_x + imag_x * imag_x) * (16.0 / math.sqrt(NFFT))
        for f in range(pairs):
            for g in range(2):
                j = 2 * f + g
                frame = i * STEP_FRAMES + f + pairs * g
                mag[pl.ds(pl.multiple_of(frame * half, half), half)] = level[
                    :, radix * j : radix * j + radix
                ]
        return carry

    steps = frames // STEP_FRAMES
    lax.fori_loop(0, steps // 2, transform, 0)
    w_line(1)
    lax.fori_loop(steps // 2, steps - 1, transform, 0)
    halo_copy.wait()
    tail = halo[...]
    ext[pl.ds(samples, halo.shape[0])] = jnp.where(me == count - 1, jnp.zeros_like(tail), tail)
    lax.fori_loop(steps - 1, steps, transform, 0)

    def regroup(m, carry):
        spec[m] = mag[pl.ds(m, frames, stride=half), :].astype(jnp.bfloat16)
        return carry

    lax.fori_loop(0, half, regroup, 0)

    def exchange(dz, dy, dc):
        target = place(lax.rem(z + dz, LINE), lax.rem(y + dy, 2), lax.rem(c + dc, 2))
        order = (dz * 2 + dy) * 2 + dc
        return send(
            spec.at[pl.ds(target * planes, planes)],
            cols.at[:, pl.ds(pl.multiple_of(me * frames, frames), frames)],
            x_send.at[order],
            x_recv.at[me],
            target,
        )

    def each_exchange(dz, act_on):
        for dy in (1, 0):
            for dc in (0, 1):
                if dz or dy or dc:
                    act_on(exchange(dz, dy, dc))

    num_h[...] = jnp.zeros_like(num_h)
    den_h[...] = jnp.zeros_like(den_h)

    def bins_plane(zz):
        span = 4 * bins
        block = wall[pl.ds(pl.multiple_of(zz * span, span), span)]
        first_plane = zz * (4 * planes)
        left = jnp.concatenate([spec[first_plane + p] for p in range(4 * planes)], axis=1)
        mid = dot(act[...], block, 1, 1).astype(jnp.bfloat16)
        num_h[...] += dot(left, block)
        den_h[...] += dot(mid, block)

    def start_exchange(point):
        for dz in EXCHANGE[point]:
            each_exchange(dz, lambda cp: cp.start())

    start_exchange(0)
    cols[:, own_frames] = spec[pl.ds(me * planes, planes)]
    w_side(0)
    w_line(2)
    start_exchange(1)
    w_plane(0, bins_plane)
    w_side(1)
    w_line(3)
    start_exchange(2)
    w_plane(1, bins_plane)
    w_side(2)
    w_plane(2, bins_plane)
    w_side(3)
    w_plane(3, bins_plane)

    h_new = (act[...].astype(jnp.float32) * num_h[...] / den_h[...]).astype(jnp.bfloat16)
    h_out[...] = h_new
    hall[own_frames] = h_new
    h_start()
    start_exchange(3)

    def exchanged(src):
        send(
            spec.at[pl.ds(0, planes)],
            cols.at[:, pl.ds(pl.multiple_of(src * frames, frames), frames)],
            x_send.at[0],
            x_recv.at[src],
            core_peer,
        ).wait_recv()

    num_w[...] = jnp.zeros_like(num_w)
    den_w[...] = jnp.zeros_like(den_w)

    def plane_rows(zz):
        span = 4 * frames
        return pl.ds(pl.multiple_of(zz * span, span), span)

    def gram_plane(zz):
        block = hall[plane_rows(zz)]
        mid = dot(wall[own_bins], block, 1, 1).astype(jnp.bfloat16)
        den_w[...] += dot(mid, block)

    def frames_plane(zz):
        rows = plane_rows(zz)
        for p in range(planes):
            num_w[pl.ds(p * radix, radix)] += dot(cols[p, rows], hall[rows], 0, 0)

    h_line(1)
    h_side(0)
    h_line(2)
    h_plane(0, gram_plane)
    h_side(1)
    h_line(3)
    h_plane(1, gram_plane)
    h_side(2)
    h_side(3)
    for dz in (0, 1, 3, 2):
        for dy in range(2):
            for dc in range(2):
                if dz or dy or dc:
                    exchanged(place(lax.rem(z + dz, LINE), lax.rem(y + dy, 2), lax.rem(c + dc, 2)))
        if dz == 0:
            frames_plane(z)
    h_plane(2, gram_plane)
    h_plane(3, gram_plane)
    for dz in (1, 3, 2):
        frames_plane(lax.rem(z + dz, LINE))
    w_out[...] = (wall[own_bins].astype(jnp.float32) * num_w[...] / den_w[...]).astype(jnp.bfloat16)
    w_drain()
    h_drain()
    for dz in range(LINE):
        each_exchange(dz, lambda cp: cp.wait_send())


def fused_shards(audio, templates, activations):
    count = lax.axis_size("row")
    frames, rank = activations.shape
    bins = templates.shape[0]
    tables = host_tables()
    aud = audio.reshape(audio.shape[0] // radix, radix)
    halo_rows = 3 * HOP // radix
    low, wide = jnp.bfloat16, jnp.float32
    vmem = pl.BlockSpec(memory_space=pltpu.VMEM)
    dma = pltpu.SemaphoreType.DMA
    return pl.pallas_call(
        fused,
        out_shape=(
            jax.ShapeDtypeStruct(activations.shape, low),
            jax.ShapeDtypeStruct(templates.shape, low),
        ),
        in_specs=[pl.BlockSpec(memory_space=pl.ANY)] * 8,
        out_specs=(vmem, vmem),
        scratch_shapes=[
            pltpu.VMEM(activations.shape, low),
            *(pltpu.VMEM(table.shape, table.dtype) for table in tables),
            pltpu.VMEM((aud.shape[0] + halo_rows, radix), low),
            pltpu.VMEM((halo_rows, radix), low),
            pltpu.VMEM((frames * BINS // radix, radix), wide),
            pltpu.VMEM((BINS // radix, frames, radix), low),
            pltpu.VMEM((bins // radix, count * frames, radix), low),
            pltpu.VMEM((count * bins, rank), low),
            pltpu.VMEM((count * frames, rank), low),
            pltpu.VMEM((frames, rank), wide),
            pltpu.VMEM((frames, rank), wide),
            pltpu.VMEM((bins, rank), wide),
            pltpu.VMEM((bins, rank), wide),
            dma((8,)),
            dma((2,)),
            dma((4, count * W_PIECES)),
            dma((count * W_PIECES,)),
            dma((4, count * H_PIECES)),
            dma((count * H_PIECES,)),
            dma((count,)),
            dma((count,)),
        ],
        compiler_params=pltpu.CompilerParams(
            collective_id=0, has_side_effects=True, vmem_limit_bytes=60 * 1024 * 1024
        ),
        cost_estimate=pl.CostEstimate(
            flops=4_000_000_000, bytes_accessed=8_000_000, transcendentals=0
        ),
        name="spectral_nmf",
    )(aud, templates, activations, *tables)


def solution(mesh):
    in_specs = (P(("parts", "row")), P(("parts", "row"), None), P(("parts", "row"), None))
    out_specs = (P(("parts", "row"), None), P(("parts", "row"), None))
    body = fused_shards if mesh.shape["row"] == LINE * 4 else shards
    return jax.shard_map(body, mesh=mesh, in_specs=in_specs, out_specs=out_specs, check_vma=False)
```

```python
import functools
import math

import jax
import jax.numpy as jnp
import numpy as np
from jax import lax
from jax.experimental import pallas as pl
from jax.experimental.pallas import tpu as pltpu
from jax.sharding import PartitionSpec as P

NFFT = 8192
BINS = 4096
HOP = 2048


radix = 128


def shifted(value, axis, by):
    length = lax.axis_size(axis)
    pairs = [(i, i + by) for i in range(length) if 0 <= i + by < length]
    return lax.ppermute(value, axis, pairs)


def dft_tables(length):
    inner_len = length // radix
    half_len = inner_len // 2
    outer_idx = jnp.arange(radix, dtype=jnp.int32)
    inner_idx = jnp.arange(inner_len, dtype=jnp.int32)
    upper_idx = jnp.arange(half_len, dtype=jnp.int32)
    angle_one = (outer_idx[:, None] * outer_idx[None, :] % radix).astype(jnp.float32) * (
        2.0 * math.pi / radix
    )
    section_one = jnp.concatenate([jnp.cos(angle_one), -jnp.sin(angle_one)], axis=1).astype(
        jnp.bfloat16
    )
    angle_twid = (inner_idx[:, None] * outer_idx[None, :] % length).astype(jnp.float32) * (
        2.0 * math.pi / length
    )
    angle_two = (inner_idx[:, None] * upper_idx[None, :] % inner_len).astype(jnp.float32) * (
        2.0 * math.pi / inner_len
    )
    cos_two = jnp.cos(angle_two)
    sin_two = jnp.sin(angle_two)
    upper_half = jnp.concatenate([cos_two, -sin_two], axis=1)
    lower_half = jnp.concatenate([sin_two, cos_two], axis=1)
    section_two = jnp.concatenate([upper_half, lower_half], axis=0).astype(jnp.bfloat16)
    sample_idx = jnp.arange(length, dtype=jnp.int32).astype(jnp.float32)
    hann_window = 0.5 - 0.5 * jnp.cos(sample_idx * (2.0 * math.pi / length))
    return (hann_window, section_one, jnp.cos(angle_twid), jnp.sin(angle_twid), section_two)


def magnitudes(windowed, tables_all):
    hann_window, section_one, twid_cos, twid_sin, section_two = tables_all
    frame_count = windowed.shape[0]
    length = windowed.shape[1]
    inner_len = section_two.shape[0] // 2
    half_len = inner_len // 2
    shaped = windowed.reshape(frame_count, radix, inner_len)
    section_out = jnp.einsum("nab,ac->nbc", shaped, section_one, preferred_element_type=jnp.float32)
    real_y = section_out[:, :, :radix]
    imag_y = section_out[:, :, radix:]
    real_z = (real_y * twid_cos + imag_y * twid_sin).astype(jnp.bfloat16)
    imag_z = (imag_y * twid_cos - real_y * twid_sin).astype(jnp.bfloat16)
    stacked = jnp.concatenate([real_z, imag_z], axis=1)
    second = jnp.einsum("nbk,bm->nmk", stacked, section_two, preferred_element_type=jnp.float32)
    real_x = second[:, :half_len, :]
    imag_x = second[:, half_len:, :]
    level = jnp.sqrt(real_x * real_x + imag_x * imag_x) * (16.0 / math.sqrt(length))
    return level.reshape(frame_count, half_len * radix).astype(jnp.bfloat16)


def inner_rows(left, right):
    return lax.dot_general(
        left, right, (((0,), (0,)), ((), ())), preferred_element_type=jnp.float32
    )


def refine(factor, numer, gram_low):
    denom = jnp.dot(factor, gram_low, preferred_element_type=jnp.float32)
    return (factor.astype(jnp.float32) * numer / denom).astype(jnp.bfloat16)


def own_gram(factor):
    return lax.psum(inner_rows(factor, factor), "row")


def shards(audio, templates, activations):
    frame_count = activations.shape[0]
    tables_all = dft_tables(NFFT)
    tail_audio = shifted(audio[: 3 * HOP], "row", -1)
    frame_rows = jnp.concatenate([audio, tail_audio]).reshape(frame_count + 3, HOP)
    block_len = math.gcd(frame_count, 16)

    def one_block(block_index):
        window_rows = lax.dynamic_slice_in_dim(
            frame_rows, block_index * block_len, block_len + 3, 0
        )
        frames = jnp.concatenate(
            [window_rows[offset : offset + block_len] for offset in range(4)], axis=1
        )
        windowed = (frames.astype(jnp.float32) * tables_all[0]).astype(jnp.bfloat16)
        return magnitudes(windowed, tables_all)

    blocks_out = lax.map(one_block, jnp.arange(frame_count // block_len, dtype=jnp.int32))
    spectrogram = blocks_out.reshape(frame_count, BINS)
    gram_w = lax.psum(inner_rows(templates, templates), "row").astype(jnp.bfloat16)
    columns = lax.all_to_all(spectrogram, "row", split_axis=1, concat_axis=0, tiled=True)
    num_h = lax.psum_scatter(
        jnp.dot(columns, templates, preferred_element_type=jnp.float32),
        "row",
        scatter_dimension=0,
        tiled=True,
    )
    h_new = refine(activations, num_h, gram_w)
    num_acc = inner_rows(columns, lax.all_gather(h_new, "row", axis=0, tiled=True))
    gram_h = own_gram(h_new)
    w_new = refine(templates, num_acc, gram_h.astype(jnp.bfloat16))
    return (h_new, w_new)


LINE = 4
STEP_FRAMES = 8
W_PIECES = 2
H_PIECES = 2
EXCHANGE = ((2,), (), (1, 3), (0,))


def host_tables():
    inner_len = NFFT // radix
    half_len = inner_len // 2
    two_pi = np.float32(2.0 * math.pi)
    outer = np.arange(radix)
    inner = np.arange(inner_len)
    upper = np.arange(half_len)
    one = (outer[:, None] * outer[None, :] % radix).astype(np.float32) * (two_pi / np.float32(radix))
    table = np.concatenate([np.cos(one), -np.sin(one)], axis=1)
    first = np.zeros((2, 2, inner_len, 2, 2 * radix), np.float32)
    for parity in range(2):
        for which in range(2):
            first[parity, which, :, which, :] = table[parity::2]
    first = first.reshape(4 * inner_len, 4 * radix)
    twid = (inner[:, None] * outer[None, :] % NFFT).astype(np.float32) * (two_pi / np.float32(NFFT))
    two = (inner[:, None] * upper[None, :] % inner_len).astype(np.float32) * (
        two_pi / np.float32(inner_len)
    )
    cos_two, sin_two = np.cos(two), np.sin(two)
    second = np.concatenate(
        [
            np.concatenate([cos_two, -sin_two], axis=1),
            np.concatenate([sin_two, cos_two], axis=1),
        ],
        axis=0,
    ).T
    samples = np.arange(NFFT).astype(np.float32)
    hann = np.float32(0.5) - np.float32(0.5) * np.cos(samples * (two_pi / np.float32(NFFT)))
    hann = hann.reshape(NFFT // radix, radix)
    return (
        jnp.asarray(np.concatenate([hann, hann], axis=0), jnp.float32),
        jnp.asarray(first).astype(jnp.bfloat16),
        jnp.asarray(np.cos(twid), jnp.float32),
        jnp.asarray(np.sin(twid), jnp.float32),
        jnp.asarray(second).astype(jnp.bfloat16),
    )


def dot(left, right, left_dim=1, right_dim=0):
    return lax.dot_general(
        left, right, (((left_dim,), (right_dim,)), ((), ())), preferred_element_type=jnp.float32
    )


def fused(
    aud_in, tmpl_in, act_in, hann_in, first_in, tcos_in, tsin_in, second_in, h_out, w_out,
    act, hann, first, tcos, tsin, second,
    ext, halo, mag, spec, cols, wall, hall, num_h, den_h, num_w, den_w,
    load_sems, halo_sems, w_send, w_recv, h_send, h_recv, x_send, x_recv,
):
    count = lax.axis_size("row")
    me = lax.axis_index("row")
    z, y, c = me // 4, (me // 2) % 2, me % 2
    frames = act_in.shape[0]
    bins = tmpl_in.shape[0]
    planes = bins // radix
    half = NFFT // radix // 2
    samples = aud_in.shape[0]

    def place(zz, yy, cc):
        return (zz * 2 + yy) * 2 + cc

    core_peer = place(z, y, 1 - c)
    y_peer = place(z, 1 - y, c)

    def send(src, dst, send_sem, recv_sem, device):
        return pltpu.make_async_remote_copy(
            src_ref=src,
            dst_ref=dst,
            send_sem=send_sem,
            recv_sem=recv_sem,
            device_id={"row": device},
            device_id_type=pl.DeviceIdType.MESH,
        )

    own_bins = pl.ds(pl.multiple_of(me * bins, bins), bins)
    own_frames = pl.ds(pl.multiple_of(me * frames, frames), frames)
    loads = [
        pltpu.make_async_copy(src, dst, load_sems.at[i])
        for i, (src, dst) in enumerate(
            (
                (tmpl_in, wall.at[own_bins]),
                (aud_in, ext.at[pl.ds(0, samples)]),
                (hann_in, hann),
                (first_in, first),
                (tcos_in, tcos),
                (tsin_in, tsin),
                (second_in, second),
                (act_in, act),
            )
        )
    ]
    for load in loads:
        load.start()

    barrier = pltpu.get_barrier_semaphore()
    for d in range(1, count):
        pl.semaphore_signal(
            barrier,
            inc=1,
            device_id={"row": lax.rem(me + d, count)},
            device_id_type=pl.DeviceIdType.MESH,
        )
    pl.semaphore_wait(barrier, count - 1)

    halo_copy = send(
        aud_in.at[pl.ds(0, halo.shape[0])], halo, halo_sems.at[0], halo_sems.at[1],
        lax.rem(me + count - 1, count),
    )
    halo_copy.start()

    def gather(buf, rows, pieces, send_sems, recv_sems):
        size = rows // pieces

        def make(slot, q, way, device):
            unit = slot * pieces + q
            view = buf.at[pl.ds(pl.multiple_of(unit * size, size), size)]
            return send(view, view, send_sems.at[way, unit], recv_sems.at[unit], device)

        def arrived(slot, q):
            make(slot, q, 0, core_peer).wait_recv()

        def each_send(slot_z, q, sign, act_on):
            slot = place(slot_z, y, c)
            for way, step in ((2, 1), (3, -1)):
                if sign in (0, step):

                    @pl.when((z + step >= 0) & (z + step < LINE))
                    def _():
                        act_on(make(slot, q, way, place(z + step, y, c)))

            act_on(make(slot, q, 1, y_peer))
            act_on(make(slot, q, 0, core_peer))

        def over_line(d, body):
            if d == 0:
                body(z, 0)
                return
            for sign in (1, -1):
                from_z = z - sign * d

                @pl.when((from_z >= 0) & (from_z < LINE))
                def _():
                    body(from_z, sign)

        def start_own():
            for q in range(pieces):
                each_send(z, q, 0, lambda cp: cp.start())

        def relay_line(d):
            for q in range(pieces):

                def body(from_z, sign):
                    arrived(place(from_z, y, c), q)
                    each_send(from_z, q, sign, lambda cp: cp.start())

                over_line(d, body)

        def relay_side(d):
            for q in range(pieces):

                def body(from_z, sign):
                    slot = place(from_z, 1 - y, c)
                    arrived(slot, q)
                    make(slot, q, 0, core_peer).start()

                over_line(d, body)

        def plane(d, process):
            def body(from_z, sign):
                for q in range(pieces):
                    for yy in range(2):
                        arrived(place(from_z, yy, 1 - c), q)
                process(from_z)

            over_line(d, body)

        def drain():
            for q in range(pieces):
                for d in range(LINE):

                    def body(from_z, sign):
                        each_send(from_z, q, sign, lambda cp: cp.wait_send())
                        make(place(from_z, 1 - y, c), q, 0, core_peer).wait_send()

                    over_line(d, body)

        return start_own, relay_line, relay_side, plane, drain

    w_start, w_line, w_side, w_plane, w_drain = gather(wall, bins, W_PIECES, w_send, w_recv)
    h_start, h_line, h_side, h_plane, h_drain = gather(hall, frames, H_PIECES, h_send, h_recv)

    loads[0].wait()
    w_start()
    for load in loads[1:]:
        load.wait()

    per_frame = HOP // radix
    pairs = STEP_FRAMES // 2

    def transform(i, carry):
        base = pl.multiple_of(i * STEP_FRAMES * per_frame, STEP_FRAMES * per_frame)
        lefts = []
        for f in range(pairs):
            block = ext[pl.ds(base + per_frame * f, radix)].astype(jnp.float32) * hann[...]
            turned = block.astype(jnp.bfloat16).T
            lefts.append(jnp.concatenate([turned[: radix // 2], turned[radix // 2 :]], axis=1))
        out_one = dot(jnp.concatenate(lefts, axis=0), first[...])
        rights = []
        for f in range(pairs):
            for g in range(2):
                piece = out_one[64 * f : 64 * f + 64, 256 * g : 256 * g + 256]
                real_y = piece[:, :radix]
                imag_y = piece[:, radix:]
                real_z = (real_y * tcos[...] + imag_y * tsin[...]).astype(jnp.bfloat16)
                imag_z = (imag_y * tcos[...] - real_y * tsin[...]).astype(jnp.bfloat16)
                rights.append(jnp.concatenate([real_z, imag_z], axis=0))
        out_two = dot(second[...], jnp.concatenate(rights, axis=1))
        real_x = out_two[:half]
        imag_x = out_two[half:]
        level = jnp.sqrt(real_x * real_x + imag_x * imag_x) * (16.0 / math.sqrt(NFFT))
        for f in range(pairs):
            for g in range(2):
                j = 2 * f + g
                frame = i * STEP_FRAMES + f + pairs * g
                mag[pl.ds(pl.multiple_of(frame * half, half), half)] = level[
                    :, radix * j : radix * j + radix
                ]
        return carry

    steps = frames // STEP_FRAMES
    lax.fori_loop(0, steps // 2, transform, 0)
    w_line(1)
    lax.fori_loop(steps // 2, steps - 1, transform, 0)
    halo_copy.wait()
    tail = halo[...]
    ext[pl.ds(samples, halo.shape[0])] = jnp.where(me == count - 1, jnp.zeros_like(tail), tail)
    lax.fori_loop(steps - 1, steps, transform, 0)

    def regroup(m, carry):
        spec[m] = mag[pl.ds(m, frames, stride=half), :].astype(jnp.bfloat16)
        return carry

    lax.fori_loop(0, half, regroup, 0)

    def exchange(dz, dy, dc):
        target = place(lax.rem(z + dz, LINE), lax.rem(y + dy, 2), lax.rem(c + dc, 2))
        order = (dz * 2 + dy) * 2 + dc
        return send(
            spec.at[pl.ds(target * planes, planes)],
            cols.at[:, pl.ds(pl.multiple_of(me * frames, frames), frames)],
            x_send.at[order],
            x_recv.at[me],
            target,
        )

    def each_exchange(dz, act_on):
        for dy in (1, 0):
            for dc in (0, 1):
                if dz or dy or dc:
                    act_on(exchange(dz, dy, dc))

    num_h[...] = jnp.zeros_like(num_h)
    den_h[...] = jnp.zeros_like(den_h)

    def bins_plane(zz):
        span = 4 * bins
        block = wall[pl.ds(pl.multiple_of(zz * span, span), span)]
        first_plane = zz * (4 * planes)
        left = jnp.concatenate([spec[first_plane + p] for p in range(4 * planes)], axis=1)
        mid = dot(act[...], block, 1, 1).astype(jnp.bfloat16)
        num_h[...] += dot(left, block)
        den_h[...] += dot(mid, block)

    def start_exchange(point):
        for dz in EXCHANGE[point]:
            each_exchange(dz, lambda cp: cp.start())

    start_exchange(0)
    cols[:, own_frames] = spec[pl.ds(me * planes, planes)]
    w_side(0)
    w_line(2)
    start_exchange(1)
    w_plane(0, bins_plane)
    w_side(1)
    w_line(3)
    start_exchange(2)
    w_plane(1, bins_plane)
    w_side(2)
    w_plane(2, bins_plane)
    w_side(3)
    w_plane(3, bins_plane)

    h_new = (act[...].astype(jnp.float32) * num_h[...] / den_h[...]).astype(jnp.bfloat16)
    h_out[...] = h_new
    hall[own_frames] = h_new
    h_start()
    start_exchange(3)

    def exchanged(src):
        send(
            spec.at[pl.ds(0, planes)],
            cols.at[:, pl.ds(pl.multiple_of(src * frames, frames), frames)],
            x_send.at[0],
            x_recv.at[src],
            core_peer,
        ).wait_recv()

    num_w[...] = jnp.zeros_like(num_w)
    den_w[...] = jnp.zeros_like(den_w)

    def plane_rows(zz):
        span = 4 * frames
        return pl.ds(pl.multiple_of(zz * span, span), span)

    def gram_plane(zz):
        block = hall[plane_rows(zz)]
        mid = dot(wall[own_bins], block, 1, 1).astype(jnp.bfloat16)
        den_w[...] += dot(mid, block)

    def frames_plane(zz):
        rows = plane_rows(zz)
        for p in range(planes):
            num_w[pl.ds(p * radix, radix)] += dot(cols[p, rows], hall[rows], 0, 0)

    h_line(1)
    h_side(0)
    h_line(2)
    h_plane(0, gram_plane)
    h_side(1)
    h_line(3)
    h_plane(1, gram_plane)
    h_side(2)
    h_plane(2, gram_plane)
    h_side(3)
    for dz in (0, 1, 3, 2):
        for dy in range(2):
            for dc in range(2):
                if dz or dy or dc:
                    exchanged(place(lax.rem(z + dz, LINE), lax.rem(y + dy, 2), lax.rem(c + dc, 2)))
        if dz == 0:
            frames_plane(z)
    h_plane(3, gram_plane)
    for dz in (1, 3, 2):
        frames_plane(lax.rem(z + dz, LINE))
    w_out[...] = (wall[own_bins].astype(jnp.float32) * num_w[...] / den_w[...]).astype(jnp.bfloat16)
    w_drain()
    h_drain()
    for dz in range(LINE):
        each_exchange(dz, lambda cp: cp.wait_send())


def fused_shards(audio, templates, activations):
    count = lax.axis_size("row")
    frames, rank = activations.shape
    bins = templates.shape[0]
    tables = host_tables()
    aud = audio.reshape(audio.shape[0] // radix, radix)
    halo_rows = 3 * HOP // radix
    low, wide = jnp.bfloat16, jnp.float32
    vmem = pl.BlockSpec(memory_space=pltpu.VMEM)
    dma = pltpu.SemaphoreType.DMA
    return pl.pallas_call(
        fused,
        out_shape=(
            jax.ShapeDtypeStruct(activations.shape, low),
            jax.ShapeDtypeStruct(templates.shape, low),
        ),
        in_specs=[pl.BlockSpec(memory_space=pl.ANY)] * 8,
        out_specs=(vmem, vmem),
        scratch_shapes=[
            pltpu.VMEM(activations.shape, low),
            *(pltpu.VMEM(table.shape, table.dtype) for table in tables),
            pltpu.VMEM((aud.shape[0] + halo_rows, radix), low),
            pltpu.VMEM((halo_rows, radix), low),
            pltpu.VMEM((frames * BINS // radix, radix), wide),
            pltpu.VMEM((BINS // radix, frames, radix), low),
            pltpu.VMEM((bins // radix, count * frames, radix), low),
            pltpu.VMEM((count * bins, rank), low),
            pltpu.VMEM((count * frames, rank), low),
            pltpu.VMEM((frames, rank), wide),
            pltpu.VMEM((frames, rank), wide),
            pltpu.VMEM((bins, rank), wide),
            pltpu.VMEM((bins, rank), wide),
            dma((8,)),
            dma((2,)),
            dma((4, count * W_PIECES)),
            dma((count * W_PIECES,)),
            dma((4, count * H_PIECES)),
            dma((count * H_PIECES,)),
            dma((count,)),
            dma((count,)),
        ],
        compiler_params=pltpu.CompilerParams(
            collective_id=0, has_side_effects=True, vmem_limit_bytes=60 * 1024 * 1024
        ),
        cost_estimate=pl.CostEstimate(
            flops=4_000_000_000, bytes_accessed=8_000_000, transcendentals=0
        ),
        name="spectral_nmf",
    )(aud, templates, activations, *tables)


def solution(mesh):
    in_specs = (P(("parts", "row")), P(("parts", "row"), None), P(("parts", "row"), None))
    out_specs = (P(("parts", "row"), None), P(("parts", "row"), None))
    body = fused_shards if mesh.shape["row"] == LINE * 4 else shards
    return jax.shard_map(body, mesh=mesh, in_specs=in_specs, out_specs=out_specs, check_vma=False)
```
